32 devices in a mesh: feat: 8 (over z, y), cand: 4 (over x, core).
Axes of the slice: x: 2, y: 2, z: 4, core: 2. Of those that a mesh axis runs over, the one named last changes fastest.
Arguments:
- cand_grads: bfloat16 [256, 1048576], P('cand', 'feat'), may hold values from -30 to 30
- val_grads: bfloat16 [64, 1048576], P('cand', 'feat'), may hold values from -30 to 30
- second_moment: float32 [1048576], P('feat'), may hold values from 0.0005 to 1.5
- slot_blocks: int32 [8, 128], replicated, may hold values from 0 to 127, as said below
- slot_seeds: int32 [8, 128], replicated, may hold values from 0 to 1073741823
Outputs:
- scores: float32 [256, 16], P('cand', 'feat')
The draws below stay inside these ranges and needn't reach their ends.
Inputs may be any that keep to these rules, and one draw needn't show every extreme that they name: `slot_blocks`: each row is a permutation of the input blocks; with L = 128 / (devices of feat), G = (devices of feat) / 8, and o_k = k * G for even k and (k - 1) * G + 1 for odd k, slot k of output block b reads an input block whose index divided by L equals (b / L + o_k) modulo the devices of feat (divisions rounded down).
All inputs are finite; a program needn't handle non-finite values.
Results may differ from the reference program's by a relative error of at most 0.0003.
Values sent between devices are 32-bit elements; how exact they have to be, the bound alone decides.
A program may use at most 128 MiB of HBM per device.

```python
import math
import jax
import jax.numpy as jnp
from jax import lax

P_SIZE = 1048576
NBLK = 128
PB = 8192
FEATS = 8192
FB = 64
SLOTS = 8
VPT = 4
CANDS = 256
NVAL = 64
TASKS = 16
N_FEAT = 8


topic_count = 8


def topic_table(key):
    base = jax.random.fold_in(key, 11)
    scale_key = jax.random.fold_in(base, 1)
    noise_key = jax.random.fold_in(base, 2)
    scales = jnp.exp(jax.random.uniform(scale_key, (topic_count, NBLK, 1), jnp.float32, math.log(0.3), math.log(3.0)))
    noise = jnp.clip(jax.random.normal(noise_key, (topic_count, NBLK, PB), jnp.float32), -5.0, 5.0)
    return (noise * scales).reshape(topic_count, P_SIZE)


def mixed_rows_keyed(key, own_key, topics, weights, count):
    table = topic_table(key)
    noise = jnp.clip(jax.random.normal(jax.random.fold_in(own_key, 14), (count, P_SIZE), jnp.float32), -6.0, 6.0)
    return (weights * jnp.take(table, topics, axis=0) + noise).astype(jnp.bfloat16)


def draw_cand_grads(key, part):
    own_key = jax.random.fold_in(key, 21)
    topics = jax.random.randint(jax.random.fold_in(own_key, 12), (CANDS,), 0, topic_count)
    weights = jax.random.uniform(jax.random.fold_in(own_key, 13), (CANDS, 1), jnp.float32, 0.4, 1.6)
    return mixed_rows_keyed(key, own_key, topics, weights, CANDS)


def draw_val_grads(key, part):
    own_key = jax.random.fold_in(key, 22)
    topics = jnp.arange(NVAL, dtype=jnp.int32) // VPT % topic_count
    weights = jax.random.uniform(jax.random.fold_in(own_key, 13), (NVAL, 1), jnp.float32, 0.6, 1.6)
    return mixed_rows_keyed(key, own_key, topics, weights, NVAL)


def draw_second_moment(key, part):
    block_key = jax.random.fold_in(key, 31)
    coord_key = jax.random.fold_in(key, 32)
    levels = jnp.exp(jax.random.uniform(block_key, (NBLK, 1), jnp.float32, math.log(0.001), math.log(1.0)))
    spread = jnp.exp(jax.random.uniform(coord_key, (NBLK, PB), jnp.float32, math.log(0.5), math.log(1.5)))
    return (levels * spread).reshape(P_SIZE)


def draw_slot_blocks(key, part):
    local_count = NBLK // N_FEAT
    stride = N_FEAT // SLOTS
    own_key = jax.random.fold_in(key, 41)
    keys = jax.random.split(own_key, SLOTS * N_FEAT)
    orders = jax.vmap(lambda one_key: jax.random.permutation(one_key, local_count))(keys)
    orders = orders.reshape(SLOTS, N_FEAT, local_count).astype(jnp.int32)
    slot_ids = jnp.arange(SLOTS, dtype=jnp.int32)[:, None]
    odd_part = slot_ids % 2
    offsets = (slot_ids - odd_part) * stride + odd_part
    owners = jnp.arange(N_FEAT, dtype=jnp.int32)[None, :]
    source = (owners + offsets) % N_FEAT
    result = source[:, :, None] * local_count + orders
    return result.reshape(SLOTS, NBLK).astype(jnp.int32)


def place_ends(entries, rng, smallest, top_value):
    index_at = [jax.random.randint(jax.random.fold_in(rng, axis), (), 0, length) for axis, length in enumerate(entries.shape)]
    widest = entries.shape.index(max(entries.shape))
    next_to = index_at[:widest] + [(index_at[widest] + 1) % entries.shape[widest]] + index_at[widest + 1:]
    return entries.at[tuple(index_at)].set(smallest).at[tuple(next_to)].set(top_value)


def setup_inputs(seed: int = 0) -> dict:
    key_list = jax.random.split(jax.random.key(seed), 6)
    cand_grads = draw_cand_grads(jax.random.fold_in(key_list[5], 71), 0)
    val_grads = draw_val_grads(jax.random.fold_in(key_list[5], 71), 0)
    second_moment = draw_second_moment(jax.random.fold_in(key_list[5], 71), 0)
    slot_blocks = draw_slot_blocks(jax.random.fold_in(key_list[5], 71), 0)
    slot_seeds = place_ends(jax.random.randint(key_list[4], (SLOTS, NBLK), 0, 1073741824), jax.random.fold_in(key_list[4], 1), 0, 1073741823).astype(jnp.int32)
    return dict(cand_grads=cand_grads, val_grads=val_grads, second_moment=second_moment, slot_blocks=slot_blocks, slot_seeds=slot_seeds)


def block_signs(seed_val, height, breadth):
    across = lax.broadcasted_iota(jnp.int32, (height, breadth), 0)
    column = lax.broadcasted_iota(jnp.int32, (height, breadth), 1)
    mixed = seed_val ^ across * jnp.int32(73856093) ^ column * jnp.int32(19349663)
    for repeat in range(2):
        mixed = mixed ^ lax.shift_right_logical(mixed, jnp.int32(16))
        mixed = mixed * jnp.int32(73244475)
    mixed = mixed ^ lax.shift_right_logical(mixed, jnp.int32(16))
    return (2 * (mixed & 1) - 1).astype(jnp.float32)

def project(rows_x, slot_blocks, slot_seeds):
    factor = 1.0 / math.sqrt(SLOTS * PB)
    height = rows_x.shape[0]

    def one_block(column):
        summed = jnp.zeros((height, FB), jnp.float32)
        for slot_no in range(SLOTS):
            offset = (slot_blocks[slot_no, column] * PB).astype(jnp.int32)
            segment = lax.dynamic_slice_in_dim(rows_x, offset, PB, 1)
            matrix = (block_signs(slot_seeds[slot_no, column], PB, FB) * factor).astype(jnp.bfloat16)
            summed = summed + jnp.dot(segment, matrix, preferred_element_type=jnp.float32)
        return summed
    blocks = lax.map(one_block, jnp.arange(NBLK, dtype=jnp.int32))
    return jnp.transpose(blocks, (1, 0, 2)).reshape(height, FEATS)

def reference(cand_grads, val_grads, second_moment, slot_blocks, slot_seeds):
    wide = cand_grads.astype(jnp.float32)
    adam_grads = (wide / (jnp.sqrt(0.999 * second_moment[None, :] + 0.001 * wide * wide) + 1e-08)).astype(jnp.bfloat16)
    cand_feats = project(adam_grads, slot_blocks, slot_seeds)
    val_feats = project(val_grads, slot_blocks, slot_seeds)
    cand_norm = jnp.sqrt(lax.optimization_barrier(jnp.sum(cand_feats * cand_feats, axis=1)) + 1e-06)
    val_norm = jnp.sqrt(lax.optimization_barrier(jnp.sum(val_feats * val_feats, axis=1)) + 1e-06)
    val_unit = val_feats / val_norm[:, None]
    dots = jnp.dot(cand_feats, val_unit.T, precision=lax.Precision.HIGHEST)
    cosine = dots / cand_norm[:, None]
    return lax.optimization_barrier(jnp.sum(cosine.reshape(CANDS, TASKS, VPT), axis=2)) / VPT
```

```python
import functools
import math

import jax
import jax.numpy as jnp
from jax import lax
from jax.experimental import pallas as pl
from jax.experimental.pallas import tpu as pltpu
from jax.sharding import PartitionSpec as P

PB = 8192
FB = 64
SLOTS = 8
VPT = 4
LANES = 128
MESH = pl.DeviceIdType.MESH
C_ROW = 73856093
C_COL = 19349663
C_MIX = 73244475
C_SIGN = ((C_MIX << 15) + (1 << 31)) & 0xFFFFFFFF
C_SIGN = C_SIGN - (1 << 32) if C_SIGN >= (1 << 31) else C_SIGN
KC = 2048
KS = 256
HIGHEST = lax.Precision.HIGHEST


def fold(h):
    return h ^ lax.shift_right_logical(h, jnp.int32(16))


def slot_shift(k, nf):
    stride = nf // SLOTS
    return k * stride if k % 2 == 0 else (k - 1) * stride + 1


def kernel(
    nf, nc, L,
    blocks_ref, seeds_ref, cand_ref, val_ref, moment_ref, out_ref,
    table, lhs, acc, prev, stage, arrived, mine, val_all, part, part_in,
    send_sem, recv_sem, val_send, val_recv, part_send, part_recv,
):
    j = pl.program_id(0)
    me = lax.axis_index("feat")
    col = lax.axis_index("cand")
    ncand = cand_ref.shape[0]
    nval = val_ref.shape[0]
    rows = ncand + nval

    @pl.when(j == 0)
    def _():
        barrier = pltpu.get_barrier_semaphore()
        for o in range(1, nf):
            pl.semaphore_signal(
                barrier, inc=1, device_id={"feat": lax.rem(me + o, nf)}, device_id_type=MESH
            )
        for o in range(1, nc):
            pl.semaphore_signal(
                barrier, inc=1, device_id={"cand": lax.rem(col + o, nc)}, device_id_type=MESH
            )

        def fill(i, carry):
            base = pl.multiple_of(i * KS, KS)
            p = lax.broadcasted_iota(jnp.int32, (KS, LANES), 0) + base
            f = lax.broadcasted_iota(jnp.int32, (KS, LANES), 1) & (FB - 1)
            table[pl.ds(base, KS), :] = fold((p * jnp.int32(C_ROW)) ^ (f * jnp.int32(C_COL)))
            return carry

        lax.fori_loop(0, PB // KS, fill, 0)

    lane = lax.broadcasted_iota(jnp.int32, (1, LANES), 1)
    low = lane < FB
    pair_seeds = []
    for q in range(SLOTS // 2):
        a = seeds_ref[2 * q, j]
        b = seeds_ref[2 * q + 1, j]
        pair_seeds.append(fold(jnp.where(low, a, b)))

    acc[...] = jnp.zeros_like(acc)

    def chunk(c, carry):
        base = pl.multiple_of(c * KC, KC)
        for s in range(KC // KS):
            here = pl.ds(base + s * KS, KS)
            wide = cand_ref[:, here].astype(jnp.float32)
            u = 0.999 * moment_ref[0, :, here] + 0.001 * (wide * wide)
            root = u * lax.rsqrt(u)
            adam = wide * pl.reciprocal(root + 1e-08, approx=True)
            lhs[:ncand, s * KS:(s + 1) * KS] = adam.astype(jnp.bfloat16)
            lhs[ncand:, s * KS:(s + 1) * KS] = val_ref[:, here]
        for h in range(SLOTS // 4):
            total = None
            for s in range(KC // KS):
                here = pl.ds(base + s * KS, KS)
                sides = []
                for q in (2 * h, 2 * h + 1):
                    x = (table[here, :] ^ pair_seeds[q]) * jnp.int32(C_MIX)
                    g = fold(x) * jnp.int32(C_SIGN)
                    sides.append(jnp.where(g < 0, 1.0, -1.0).astype(jnp.bfloat16))
                signs = jnp.concatenate(sides, axis=1)
                product = jnp.dot(
                    lhs[:, s * KS:(s + 1) * KS], signs, preferred_element_type=jnp.float32
                )
                total = product if total is None else total + product
            acc[:, h * 256:(h + 1) * 256] += total
        return carry

    lax.fori_loop(0, PB // KC, chunk, 0)

    odd = lax.rem(j, 2) == 1

    @pl.when(jnp.logical_not(odd))
    def _():
        prev[...] = acc[...]

    @pl.when(j == 1)
    def _():
        pl.semaphore_wait(pltpu.get_barrier_semaphore(), nf + nc - 2)

    def feature_copy(k, pair):
        return pltpu.make_async_remote_copy(
            src_ref=stage.at[k, pair],
            dst_ref=arrived.at[k, pair],
            send_sem=send_sem.at[k],
            recv_sem=recv_sem.at[k],
            device_id={"feat": lax.rem(me + nf - slot_shift(k, nf), nf)},
            device_id_type=MESH,
        )

    @pl.when(odd)
    def _():
        pair = lax.div(j, 2)
        for q in range(SLOTS // 2):
            first = prev[:, q * LANES:(q + 1) * LANES]
            second = acc[:, q * LANES:(q + 1) * LANES]
            stage[2 * q, pair] = jnp.where(low, first, pltpu.roll(second, FB, 1))
            stage[2 * q + 1, pair] = jnp.where(low, pltpu.roll(first, FB, 1), second)
        for k in range(1, SLOTS):
            feature_copy(k, pair).start()

    @pl.when(j == L - 1)
    def _():
        for k in range(1, SLOTS):
            pltpu.make_async_remote_copy(
                src_ref=stage.at[k],
                dst_ref=arrived.at[k],
                send_sem=send_sem.at[k],
                recv_sem=recv_sem.at[k],
                device_id={"feat": lax.rem(me + nf - slot_shift(k, nf), nf)},
                device_id_type=MESH,
            ).wait()
        factor = 1.0 / math.sqrt(SLOTS * PB)
        for i in range(L // 2):
            total = None
            for k in range(SLOTS):
                j0 = lax.rem(blocks_ref[k, me * L + 2 * i], jnp.int32(L))
                j1 = lax.rem(blocks_ref[k, me * L + 2 * i + 1], jnp.int32(L))
                held = stage if k == 0 else arrived
                x = held[k, lax.shift_right_logical(j0, jnp.int32(1))]
                y = held[k, lax.shift_right_logical(j1, jnp.int32(1))]
                take_x = jnp.broadcast_to(j0 & 1, (1, LANES)) == 0
                take_y = jnp.broadcast_to(j1 & 1, (1, LANES)) == 1
                x = jnp.where(take_x, x, pltpu.roll(x, FB, 1))
                y = jnp.where(take_y, y, pltpu.roll(y, FB, 1))
                both = jnp.where(low, x, y)
                total = both if total is None else total + both
            total = total * factor
            mine[:, i * LANES:(i + 1) * LANES] = total[:ncand]
            val_all[col, :, i * LANES:(i + 1) * LANES] = total[ncand:]

        def val_copy(o):
            return pltpu.make_async_remote_copy(
                src_ref=val_all.at[col],
                dst_ref=val_all.at[col],
                send_sem=val_send.at[o],
                recv_sem=val_recv.at[o],
                device_id={"cand": lax.rem(col + o, nc)},
                device_id_type=MESH,
            )

        for o in range(1, nc):
            val_copy(o).start()
        feats = mine[...]
        ones = jnp.ones((8, L * FB), jnp.float32)
        contract = (((1,), (1,)), ((), ()))
        cand_sq = lax.dot_general(
            ones, feats * feats, contract, precision=HIGHEST, preferred_element_type=jnp.float32
        )
        for o in range(1, nc):
            val_copy(o).wait()
        vals = val_all[...].reshape(nc * nval, L * FB)
        dots = lax.dot_general(
            vals, feats, contract, precision=HIGHEST, preferred_element_type=jnp.float32
        )
        val_sq = jnp.sum(vals * vals, axis=1, keepdims=True)
        vrows = nc * nval // nf
        for t in range(nf):
            here = slice(t * vrows, (t + 1) * vrows)
            part[t, :vrows, :ncand] = dots[here]
            part[t, :vrows, ncand:] = jnp.broadcast_to(val_sq[here], (vrows, LANES - ncand))
            part[t, vrows:, :ncand] = cand_sq
            part[t, vrows:, ncand:] = jnp.zeros((8, LANES - ncand), jnp.float32)

        def part_copy(o):
            to = lax.rem(me + o, nf)
            return pltpu.make_async_remote_copy(
                src_ref=part.at[to],
                dst_ref=part_in.at[o],
                send_sem=part_send.at[o],
                recv_sem=part_recv.at[o],
                device_id={"feat": to},
                device_id_type=MESH,
            )

        for o in range(1, nf):
            part_copy(o).start()
        total = part[me]
        for o in range(1, nf):
            part_copy(o).wait()
            total = total + part_in[o]
        unit = total[:vrows, :ncand] / jnp.sqrt(total[:vrows, ncand:2 * ncand] + 1e-06)
        norm = jnp.sqrt(total[vrows:vrows + 1, :ncand] + 1e-06)
        for t in range(vrows // VPT):
            summed = jnp.sum(unit[t * VPT:(t + 1) * VPT], axis=0, keepdims=True)
            out_ref[t:t + 1, :] = summed / VPT / norm


def body(nf, nc, cand_grads, val_grads, second_moment, slot_blocks, slot_seeds):
    L = second_moment.shape[0] // PB
    ncand, nval = cand_grads.shape[0], val_grads.shape[0]
    rows = ncand + nval
    first = lax.axis_index("feat") * L
    local = first + jnp.arange(L, dtype=jnp.int32)
    matches = slot_blocks[:, None, :] == local[None, :, None]
    seeds = jnp.sum(jnp.where(matches, slot_seeds[:, None, :], 0), axis=2)
    vrows = nc * nval // nf
    f32, bf16, i32 = jnp.float32, jnp.bfloat16, jnp.int32
    VMEM, DMA = pltpu.VMEM, pltpu.SemaphoreType.DMA
    out = pl.pallas_call(
        functools.partial(kernel, nf, nc, L),
        out_shape=jax.ShapeDtypeStruct((vrows // VPT, ncand), f32),
        grid=(L,),
        in_specs=[
            pl.BlockSpec(memory_space=pltpu.SMEM),
            pl.BlockSpec(memory_space=pltpu.SMEM),
            pl.BlockSpec((ncand, PB), lambda j: (0, j)),
            pl.BlockSpec((nval, PB), lambda j: (0, j)),
            pl.BlockSpec((1, 1, PB), lambda j: (j, 0, 0)),
        ],
        out_specs=pl.BlockSpec((vrows // VPT, ncand), lambda j: (0, 0)),
        scratch_shapes=[
            VMEM((PB, LANES), i32),
            VMEM((rows, KC), bf16),
            VMEM((rows, SLOTS * FB), f32),
            VMEM((rows, SLOTS * FB), f32),
            VMEM((SLOTS, L // 2, rows, LANES), f32),
            VMEM((SLOTS, L // 2, rows, LANES), f32),
            VMEM((ncand, L * FB), f32),
            VMEM((nc, nval, L * FB), f32),
            VMEM((nf, vrows + 8, LANES), f32),
            VMEM((nf, vrows + 8, LANES), f32),
            DMA((SLOTS,)), DMA((SLOTS,)),
            DMA((nc,)), DMA((nc,)),
            DMA((nf,)), DMA((nf,)),
        ],
        compiler_params=pltpu.CompilerParams(
            collective_id=0, has_side_effects=True, vmem_limit_bytes=48 * 1024 * 1024,
            dimension_semantics=("arbitrary",),
        ),
        cost_estimate=pl.CostEstimate(
            flops=2 * rows * L * PB * SLOTS * FB, bytes_accessed=2 * rows * L * PB, transcendentals=0
        ),
    )(slot_blocks, seeds, cand_grads, val_grads, second_moment.reshape(L, 1, PB))
    return out.T


def solution(mesh):
    placed = (P("cand", "feat"), P("cand", "feat"), P("feat"), P(), P())
    return jax.shard_map(
        functools.partial(body, mesh.shape["feat"], mesh.shape["cand"]),
        mesh=mesh, in_specs=placed, out_specs=P("cand", "feat"), check_vma=False,
    )
```

```python
import functools
import math

import jax
import jax.numpy as jnp
from jax import lax
from jax.experimental import pallas as pl
from jax.experimental.pallas import tpu as pltpu
from jax.sharding import PartitionSpec as P

PB = 8192
FB = 64
SLOTS = 8
VPT = 4
LANES = 128
MESH = pl.DeviceIdType.MESH
C_ROW = 73856093
C_COL = 19349663
C_MIX = 73244475
C_SIGN = ((C_MIX << 15) + (1 << 31)) & 0xFFFFFFFF
C_SIGN = C_SIGN - (1 << 32) if C_SIGN >= (1 << 31) else C_SIGN
KC = 2048
KS = 256
HIGHEST = lax.Precision.HIGHEST


def fold(h):
    return h ^ lax.shift_right_logical(h, jnp.int32(16))


def slot_shift(k, nf):
    stride = nf // SLOTS
    return k * stride if k % 2 == 0 else (k - 1) * stride + 1


def kernel(
    nf, nc, L,
    blocks_ref, seeds_ref, cand_ref, val_ref, moment_ref, out_ref,
    table, lhs, own, outgoing, incoming, acc, prev, stage, arrived, mine, val_all, part, part_in,
    grad_send, grad_recv, send_sem, recv_sem, val_send, val_recv, part_send, part_recv,
):
    i = pl.program_id(0)
    steps = L // 2
    pairs = L // 4
    me = lax.axis_index("feat")
    col = lax.axis_index("cand")
    core = lax.rem(col, 2)
    other = col + 1 - 2 * core
    ncand = cand_ref.shape[0]
    nval = val_ref.shape[0]
    rows = ncand + nval
    nch = PB // KC

    @pl.when(i == 0)
    def _():
        barrier = pltpu.get_barrier_semaphore()
        for o in range(1, nc):
            pl.semaphore_signal(
                barrier, inc=1, device_id={"cand": lax.rem(col + o, nc)}, device_id_type=MESH
            )
        for o in range(1, nf):
            for c in (col, other):
                pl.semaphore_signal(
                    barrier, inc=1, device_id={"feat": lax.rem(me + o, nf), "cand": c},
                    device_id_type=MESH,
                )

        def fill(r, carry):
            base = pl.multiple_of(r * KS, KS)
            p = lax.broadcasted_iota(jnp.int32, (KS, LANES), 0) + base
            f = lax.broadcasted_iota(jnp.int32, (KS, LANES), 1) & (FB - 1)
            table[pl.ds(base, KS), :] = fold((p * jnp.int32(C_ROW)) ^ (f * jnp.int32(C_COL)))
            return carry

        lax.fori_loop(0, PB // KS, fill, 0)
        pl.semaphore_wait(barrier, 2 * (nf - 1) + nc - 1)

    lane = lax.broadcasted_iota(jnp.int32, (1, LANES), 1)
    low = lane < FB

    def adam_part(block, here):
        at = pl.ds(pl.multiple_of(block * PB + here, KS), KS)
        wide = cand_ref[:, at].astype(jnp.float32)
        u = 0.999 * moment_ref[0, :, at] + 0.001 * (wide * wide)
        root = u * lax.rsqrt(u)
        adam = wide * pl.reciprocal(root + 1e-08, approx=True)
        return adam.astype(jnp.bfloat16), val_ref[:, at]

    def grad_copy(slot, c):
        src = outgoing.at[slot] if c is None else outgoing.at[slot, c]
        dst = incoming.at[i] if c is None else incoming.at[i, c]
        return pltpu.make_async_remote_copy(
            src_ref=src, dst_ref=dst,
            send_sem=grad_send.at[slot], recv_sem=grad_recv.at[i],
            device_id={"cand": other}, device_id_type=MESH,
        )

    def whole_grad(step):
        slot = lax.rem(step, 2)
        return pltpu.make_async_remote_copy(
            src_ref=outgoing.at[slot], dst_ref=incoming.at[step],
            send_sem=grad_send.at[slot], recv_sem=grad_recv.at[step],
            device_id={"cand": other}, device_id_type=MESH,
        )

    def feature_copy(k, t, pair):
        src = stage.at[k, t] if pair is None else stage.at[k, t, pair]
        dst = arrived.at[k, core] if pair is None else arrived.at[k, core, pair]
        to = lax.rem(me + nf - slot_shift(k, nf), nf)
        return pltpu.make_async_remote_copy(
            src_ref=src, dst_ref=dst,
            send_sem=send_sem.at[k, t], recv_sem=recv_sem.at[k, core],
            device_id={"feat": to, "cand": other if t else col}, device_id_type=MESH,
        )

    @pl.when(i < steps)
    def _():
        slot = lax.rem(i, 2)

        @pl.when(i >= 2)
        def _():
            whole_grad(i - 2).wait_send()

        def give(c, carry):
            for s in range(KC // KS):
                here = slice(s * KS, (s + 1) * KS)
                adam, val = adam_part(1 - core, c * KC + s * KS)
                outgoing[slot, c, :ncand, here] = adam.astype(jnp.float32)
                outgoing[slot, c, ncand:, here] = val.astype(jnp.float32)
            grad_copy(slot, c).start()
            return carry

        def keep(c, carry):
            for s in range(KC // KS):
                here = slice(s * KS, (s + 1) * KS)
                adam, val = adam_part(core, c * KC + s * KS)
                own[slot, c, :ncand, here] = adam
                own[slot, c, ncand:, here] = val
            return carry

        lax.fori_loop(0, nch, give, 0)
        lax.fori_loop(0, nch, keep, 0)

    @pl.when(i > 0)
    def _():
        step = i - 1
        block = 2 * step + core
        slot = lax.rem(step, 2)
        pair_seeds = []
        for q in range(SLOTS // 2):
            a = seeds_ref[2 * q, block]
            b = seeds_ref[2 * q + 1, block]
            pair_seeds.append(fold(jnp.where(low, a, b)))

        acc[...] = jnp.zeros_like(acc)
        whole_grad(step).wait_recv()

        def chunk(c, carry):
            base = pl.multiple_of(c * KC, KC)
            lhs[:rows] = own[slot, c]
            lhs[rows:] = incoming[step, c].astype(jnp.bfloat16)
            for h in range(SLOTS // 4):
                total = None
                for s in range(KC // KS):
                    here = pl.ds(base + s * KS, KS)
                    sides = []
                    for q in (2 * h, 2 * h + 1):
                        x = (table[here, :] ^ pair_seeds[q]) * jnp.int32(C_MIX)
                        g = fold(x) * jnp.int32(C_SIGN)
                        sides.append(jnp.where(g < 0, 1.0, -1.0).astype(jnp.bfloat16))
                    signs = jnp.concatenate(sides, axis=1)
                    product = jnp.dot(
                        lhs[:, s * KS:(s + 1) * KS], signs, preferred_element_type=jnp.float32
                    )
                    total = product if total is None else total + product
                acc[:, h * 256:(h + 1) * 256] += total
            return carry

        lax.fori_loop(0, nch, chunk, 0)
        odd = lax.rem(step, 2) == 1

        @pl.when(jnp.logical_not(odd))
        def _():
            prev[...] = acc[...]

        @pl.when(odd)
        def _():
            pair = lax.div(step, 2)
            for q in range(SLOTS // 2):
                first = prev[:, q * LANES:(q + 1) * LANES]
                second = acc[:, q * LANES:(q + 1) * LANES]
                even_slot = jnp.where(low, first, pltpu.roll(second, FB, 1))
                odd_slot = jnp.where(low, pltpu.roll(first, FB, 1), second)
                for k, full in ((2 * q, even_slot), (2 * q + 1, odd_slot)):
                    if k == 0:
                        arrived[k, core, pair] = full[:rows]
                    else:
                        stage[k, 0, pair] = full[:rows]
                    stage[k, 1, pair] = full[rows:]
            for k in range(SLOTS):
                for t in (0, 1):
                    if k or t:
                        feature_copy(k, t, pair).start()

    def feature_wait(k, c):
        pltpu.make_async_remote_copy(
            src_ref=stage.at[k, 1], dst_ref=arrived.at[k, c],
            send_sem=send_sem.at[k, 1], recv_sem=recv_sem.at[k, c],
            device_id={"cand": other}, device_id_type=MESH,
        ).wait_recv()

    @pl.when(i == steps)
    def _():
        whole_grad(steps - 2).wait_send()
        whole_grad(steps - 1).wait_send()
        for k in range(SLOTS):
            for t in (0, 1):
                if k or t:
                    feature_copy(k, t, None).wait_send()
            if k:
                feature_wait(k, core)
            feature_wait(k, 1 - core)
        factor = 1.0 / math.sqrt(SLOTS * PB)
        for i in range(L // 2):
            total = None
            for k in range(SLOTS):
                j0 = lax.rem(blocks_ref[k, me * L + 2 * i], jnp.int32(L))
                j1 = lax.rem(blocks_ref[k, me * L + 2 * i + 1], jnp.int32(L))
                x = arrived[k, j0 & 1, lax.shift_right_logical(j0, jnp.int32(2))]
                y = arrived[k, j1 & 1, lax.shift_right_logical(j1, jnp.int32(2))]
                take_x = jnp.broadcast_to(j0 & 2, (1, LANES)) == 0
                take_y = jnp.broadcast_to(j1 & 2, (1, LANES)) == 2
                x = jnp.where(take_x, x, pltpu.roll(x, FB, 1))
                y = jnp.where(take_y, y, pltpu.roll(y, FB, 1))
                both = jnp.where(low, x, y)
                total = both if total is None else total + both
            total = total * factor
            mine[:, i * LANES:(i + 1) * LANES] = total[:ncand]
            val_all[col, :, i * LANES:(i + 1) * LANES] = total[ncand:]

        def val_copy(o):
            return pltpu.make_async_remote_copy(
                src_ref=val_all.at[col],
                dst_ref=val_all.at[col],
                send_sem=val_send.at[o],
                recv_sem=val_recv.at[o],
                device_id={"cand": lax.rem(col + o, nc)},
                device_id_type=MESH,
            )

        for o in range(1, nc):
            val_copy(o).start()
        feats = mine[...]
        ones = jnp.ones((8, L * FB), jnp.float32)
        contract = (((1,), (1,)), ((), ()))
        cand_sq = lax.dot_general(
            ones, feats * feats, contract, precision=HIGHEST, preferred_element_type=jnp.float32
        )
        for o in range(1, nc):
            val_copy(o).wait()
        vals = val_all[...].reshape(nc * nval, L * FB)
        dots = lax.dot_general(
            vals, feats, contract, precision=HIGHEST, preferred_element_type=jnp.float32
        )
        val_sq = jnp.sum(vals * vals, axis=1, keepdims=True)
        vrows = nc * nval // nf
        for t in range(nf):
            here = slice(t * vrows, (t + 1) * vrows)
            part[t, :vrows, :ncand] = dots[here]
            part[t, :vrows, ncand:] = jnp.broadcast_to(val_sq[here], (vrows, LANES - ncand))
            part[t, vrows:, :ncand] = cand_sq
            part[t, vrows:, ncand:] = jnp.zeros((8, LANES - ncand), jnp.float32)

        def part_copy(o):
            to = lax.rem(me + o, nf)
            return pltpu.make_async_remote_copy(
                src_ref=part.at[to],
                dst_ref=part_in.at[o],
                send_sem=part_send.at[o],
                recv_sem=part_recv.at[o],
                device_id={"feat": to},
                device_id_type=MESH,
            )

        for o in range(1, nf):
            part_copy(o).start()
        total = part[me]
        for o in range(1, nf):
            part_copy(o).wait()
            total = total + part_in[o]
        unit = total[:vrows, :ncand] / jnp.sqrt(total[:vrows, ncand:2 * ncand] + 1e-06)
        norm = jnp.sqrt(total[vrows:vrows + 1, :ncand] + 1e-06)
        for t in range(vrows // VPT):
            summed = jnp.sum(unit[t * VPT:(t + 1) * VPT], axis=0, keepdims=True)
            out_ref[t:t + 1, :] = summed / VPT / norm


def body(nf, nc, cand_grads, val_grads, second_moment, slot_blocks, slot_seeds):
    L = second_moment.shape[0] // PB
    ncand, nval = cand_grads.shape[0], val_grads.shape[0]
    rows = ncand + nval
    first = lax.axis_index("feat") * L
    local = first + jnp.arange(L, dtype=jnp.int32)
    matches = slot_blocks[:, None, :] == local[None, :, None]
    seeds = jnp.sum(jnp.where(matches, slot_seeds[:, None, :], 0), axis=2)
    vrows = nc * nval // nf
    steps = L // 2
    f32, bf16, i32 = jnp.float32, jnp.bfloat16, jnp.int32
    VMEM, DMA = pltpu.VMEM, pltpu.SemaphoreType.DMA
    out = pl.pallas_call(
        functools.partial(kernel, nf, nc, L),
        out_shape=jax.ShapeDtypeStruct((vrows // VPT, ncand), f32),
        grid=(steps + 1,),
        in_specs=[
            pl.BlockSpec(memory_space=pltpu.SMEM),
            pl.BlockSpec(memory_space=pltpu.SMEM),
            pl.BlockSpec((ncand, 2 * PB), lambda i: (0, jnp.minimum(i, steps - 1))),
            pl.BlockSpec((nval, 2 * PB), lambda i: (0, jnp.minimum(i, steps - 1))),
            pl.BlockSpec((1, 1, 2 * PB), lambda i: (jnp.minimum(i, steps - 1), 0, 0)),
        ],
        out_specs=pl.BlockSpec((vrows // VPT, ncand), lambda i: (0, 0)),
        scratch_shapes=[
            VMEM((PB, LANES), i32),
            VMEM((2 * rows, KC), bf16),
            VMEM((2, PB // KC, rows, KC), bf16),
            VMEM((2, PB // KC, rows, KC), f32),
            VMEM((steps, PB // KC, rows, KC), f32),
            VMEM((2 * rows, SLOTS * FB), f32),
            VMEM((2 * rows, SLOTS * FB), f32),
            VMEM((SLOTS, 2, L // 4, rows, LANES), f32),
            VMEM((SLOTS, 2, L // 4, rows, LANES), f32),
            VMEM((ncand, L * FB), f32),
            VMEM((nc, nval, L * FB), f32),
            VMEM((nf, vrows + 8, LANES), f32),
            VMEM((nf, vrows + 8, LANES), f32),
            DMA((2,)), DMA((steps,)),
            DMA((SLOTS, 2)), DMA((SLOTS, 2)),
            DMA((nc,)), DMA((nc,)),
            DMA((nf,)), DMA((nf,)),
        ],
        compiler_params=pltpu.CompilerParams(
            collective_id=0, has_side_effects=True, vmem_limit_bytes=56 * 1024 * 1024,
            dimension_semantics=("arbitrary",),
        ),
        cost_estimate=pl.CostEstimate(
            flops=2 * rows * L * PB * SLOTS * FB, bytes_accessed=2 * rows * L * PB, transcendentals=0
        ),
    )(slot_blocks, seeds, cand_grads, val_grads, second_moment.reshape(steps, 1, 2 * PB))
    return out.T


def solution(mesh):
    placed = (P("cand", "feat"), P("cand", "feat"), P("feat"), P(), P())
    return jax.shard_map(
        functools.partial(body, mesh.shape["feat"], mesh.shape["cand"]),
        mesh=mesh, in_specs=placed, out_specs=P("cand", "feat"), check_vma=False,
    )
```

```python
import functools
import math

import jax
import jax.numpy as jnp
from jax import lax
from jax.experimental import pallas as pl
from jax.experimental.pallas import tpu as pltpu
from jax.sharding import PartitionSpec as P

PB = 8192
FB = 64
SLOTS = 8
VPT = 4
LANES = 128
MESH = pl.DeviceIdType.MESH
C_ROW = 73856093
C_COL = 19349663
C_MIX = 73244475
C_SIGN = ((C_MIX << 15) + (1 << 31)) & 0xFFFFFFFF
C_SIGN = C_SIGN - (1 << 32) if C_SIGN >= (1 << 31) else C_SIGN
KC = 2048
KS = 256
HIGHEST = lax.Precision.HIGHEST


def fold(h):
    return h ^ lax.shift_right_logical(h, jnp.int32(16))


def slot_shift(k, nf):
    stride = nf // SLOTS
    return k * stride if k % 2 == 0 else (k - 1) * stride + 1


def kernel(
    nf, nc, L,
    blocks_ref, map_ref, seeds_ref, cand_ref, val_ref, moment_ref, out_ref,
    table, lhs, own, outgoing, incoming, acc, stage, arrived, mine, val_all, part, part_in,
    grad_send, grad_recv, send_sem, recv_sem, val_send, val_recv, part_send, part_recv,
):
    i = pl.program_id(0)
    steps = L // 2
    me = lax.axis_index("feat")
    col = lax.axis_index("cand")
    core = lax.rem(col, 2)
    other = col + 1 - 2 * core
    ncand = cand_ref.shape[0]
    nval = val_ref.shape[0]
    rows = ncand + nval
    nch = PB // KC

    @pl.when(i == 0)
    def _():
        barrier = pltpu.get_barrier_semaphore()
        for o in range(1, nc):
            pl.semaphore_signal(
                barrier, inc=1, device_id={"cand": lax.rem(col + o, nc)}, device_id_type=MESH
            )
        for o in range(1, nf):
            for c in (col, other):
                pl.semaphore_signal(
                    barrier, inc=1, device_id={"feat": lax.rem(me + o, nf), "cand": c},
                    device_id_type=MESH,
                )

        pl.semaphore_wait(barrier, 2 * (nf - 1) + nc - 1)

    lane = lax.broadcasted_iota(jnp.int32, (1, LANES), 1)
    low = lane < FB

    def adam_part(block, here):
        at = pl.ds(pl.multiple_of(block * PB + here, KS), KS)
        wide = cand_ref[:, at].astype(jnp.float32)
        u = 0.999 * moment_ref[0, :, at] + 0.001 * (wide * wide)
        root = u * lax.rsqrt(u)
        adam = wide * pl.reciprocal(root + 1e-08, approx=True)
        return adam.astype(jnp.bfloat16), val_ref[:, at]

    def grad_copy(step, c):
        slot = lax.rem(step, 2)
        return pltpu.make_async_remote_copy(
            src_ref=outgoing.at[slot, c], dst_ref=incoming.at[step, c],
            send_sem=grad_send.at[slot], recv_sem=grad_recv.at[step, c],
            device_id={"cand": other}, device_id_type=MESH,
        )

    def whole_grad(step):
        slot = lax.rem(step, 2)
        return pltpu.make_async_remote_copy(
            src_ref=outgoing.at[slot], dst_ref=incoming.at[step],
            send_sem=grad_send.at[slot], recv_sem=grad_recv.at[step, 0],
            device_id={"cand": other}, device_id_type=MESH,
        )

    def feature_copy(k, t, pair):
        src = stage.at[k, t] if pair is None else stage.at[k, t, pair]
        dst = arrived.at[k, core] if pair is None else arrived.at[k, core, pair]
        to = lax.rem(me + nf - slot_shift(k, nf), nf)
        return pltpu.make_async_remote_copy(
            src_ref=src, dst_ref=dst,
            send_sem=send_sem.at[k, t], recv_sem=recv_sem.at[k, core],
            device_id={"feat": to, "cand": other if t else col}, device_id_type=MESH,
        )

    @pl.when(i < steps)
    def _():
        slot = lax.rem(i, 2)

        @pl.when(i >= 2)
        def _():
            whole_grad(i - 2).wait_send()

        def give(c, carry):
            for s in range(KC // KS):
                here = slice(s * KS, (s + 1) * KS)
                adam, val = adam_part(1 - core, c * KC + s * KS)
                outgoing[slot, c, :ncand, here] = adam.astype(jnp.float32)
                outgoing[slot, c, ncand:, here] = val.astype(jnp.float32)
            grad_copy(i, c).start()
            return carry

        def keep(c, carry):
            for s in range(KC // KS):
                here = slice(s * KS, (s + 1) * KS)
                adam, val = adam_part(core, c * KC + s * KS)
                own[slot, c, :ncand, here] = adam
                own[slot, c, ncand:, here] = val
            return carry

        lax.fori_loop(0, nch, give, 0)

        @pl.when(i == 0)
        def _():
            def fill(r, carry):
                base = pl.multiple_of(r * KS, KS)
                p = lax.broadcasted_iota(jnp.int32, (KS, LANES), 0) + base
                f = lax.broadcasted_iota(jnp.int32, (KS, LANES), 1) & (FB - 1)
                table[pl.ds(base, KS), :] = fold((p * jnp.int32(C_ROW)) ^ (f * jnp.int32(C_COL)))
                return carry

            lax.fori_loop(0, PB // KS, fill, 0)

        lax.fori_loop(0, nch, keep, 0)

    @pl.when(i > 0)
    def _():
        step = i - 1
        block = 2 * step + core
        slot = lax.rem(step, 2)
        found = map_ref[...] == me * L + block
        picked = jnp.sum(jnp.where(found, seeds_ref[...], 0), axis=1, keepdims=True)
        picked = jnp.broadcast_to(picked, (SLOTS, LANES))
        pair_seeds = []
        for q in range(SLOTS // 2):
            a = picked[2 * q:2 * q + 1]
            b = picked[2 * q + 1:2 * q + 2]
            pair_seeds.append(fold(jnp.where(low, a, b)))

        acc[...] = jnp.zeros_like(acc)

        for h in range(SLOTS // 4):
            def chunk(c, carry):
                base = pl.multiple_of(c * KC, KC)
                if h == 0:
                    grad_copy(step, c).wait_recv()
                    lhs[c, :rows] = own[slot, c]
                    lhs[c, rows:] = incoming[step, c].astype(jnp.bfloat16)
                total = None
                for s in range(KC // KS):
                    here = pl.ds(base + s * KS, KS)
                    sides = []
                    for q in (2 * h, 2 * h + 1):
                        x = (table[here, :] ^ pair_seeds[q]) * jnp.int32(C_MIX)
                        g = fold(x) * jnp.int32(C_SIGN)
                        sides.append(jnp.where(g < 0, 1.0, -1.0).astype(jnp.bfloat16))
                    signs = jnp.concatenate(sides, axis=1)
                    product = jnp.dot(
                        lhs[c, :, s * KS:(s + 1) * KS], signs, preferred_element_type=jnp.float32
                    )
                    total = product if total is None else total + product
                acc[:, h * 256:(h + 1) * 256] += total
                return carry

            lax.fori_loop(0, nch, chunk, 0)
            for q in (2 * h, 2 * h + 1):
                both = acc[:, q * LANES:(q + 1) * LANES]
                turned = pltpu.roll(both, FB, 1)
                for t in (0, 1):
                    top = slice(t * rows, t * rows + rows // 2)
                    end = slice(t * rows + rows // 2, (t + 1) * rows)
                    even_slot = jnp.where(low, both[top], turned[end])
                    odd_slot = jnp.where(low, turned[top], both[end])
                    for k, folded in ((2 * q, even_slot), (2 * q + 1, odd_slot)):
                        if k or t:
                            stage[k, t, step] = folded
                        else:
                            arrived[k, core, step] = folded
            for k in range(4 * h, 4 * h + 4):
                for t in (0, 1):
                    if k or t:
                        feature_copy(k, t, step).start()

    def feature_wait(k, c):
        pltpu.make_async_remote_copy(
            src_ref=stage.at[k, 1], dst_ref=arrived.at[k, c],
            send_sem=send_sem.at[k, 1], recv_sem=recv_sem.at[k, c],
            device_id={"cand": other}, device_id_type=MESH,
        ).wait_recv()

    @pl.when(i == steps)
    def _():
        whole_grad(steps - 2).wait_send()
        whole_grad(steps - 1).wait_send()
        for k in range(SLOTS):
            for t in (0, 1):
                if k or t:
                    feature_copy(k, t, None).wait_send()
            if k:
                feature_wait(k, core)
            feature_wait(k, 1 - core)
        factor = 1.0 / math.sqrt(SLOTS * PB)
        for n in range(L // 2):
            sums = []
            for b in (2 * n, 2 * n + 1):
                total = None
                for k in range(SLOTS):
                    at = lax.rem(blocks_ref[k, me * L + b], jnp.int32(L))
                    term = arrived[k, at & 1, lax.shift_right_logical(at, jnp.int32(1))]
                    total = term if total is None else total + term
                sums.append(total * factor)
            top = jnp.where(low, sums[0], pltpu.roll(sums[1], FB, 1))
            end = jnp.where(low, pltpu.roll(sums[0], FB, 1), sums[1])
            here = slice(n * LANES, (n + 1) * LANES)
            mine[:rows // 2, here] = top
            mine[rows // 2:, here] = end[:ncand - rows // 2]
            val_all[col, :, here] = end[ncand - rows // 2:]

        def val_copy(o):
            return pltpu.make_async_remote_copy(
                src_ref=val_all.at[col],
                dst_ref=val_all.at[col],
                send_sem=val_send.at[o],
                recv_sem=val_recv.at[o],
                device_id={"cand": lax.rem(col + o, nc)},
                device_id_type=MESH,
            )

        for o in range(1, nc):
            val_copy(o).start()
        feats = mine[...]
        ones = jnp.ones((8, L * FB), jnp.float32)
        contract = (((1,), (1,)), ((), ()))
        cand_sq = lax.dot_general(
            ones, feats * feats, contract, precision=HIGHEST, preferred_element_type=jnp.float32
        )
        for o in range(1, nc):
            val_copy(o).wait()
        vals = val_all[...].reshape(nc * nval, L * FB)
        dots = lax.dot_general(
            vals, feats, contract, precision=HIGHEST, preferred_element_type=jnp.float32
        )
        val_sq = jnp.sum(vals * vals, axis=1, keepdims=True)
        vrows = nc * nval // nf
        for t in range(nf):
            here = slice(t * vrows, (t + 1) * vrows)
            part[t, :vrows, :ncand] = dots[here]
            part[t, :vrows, ncand:] = jnp.broadcast_to(val_sq[here], (vrows, LANES - ncand))
            part[t, vrows:, :ncand] = cand_sq
            part[t, vrows:, ncand:] = jnp.zeros((8, LANES - ncand), jnp.float32)

        def part_copy(o):
            to = lax.rem(me + o, nf)
            return pltpu.make_async_remote_copy(
                src_ref=part.at[to],
                dst_ref=part_in.at[o],
                send_sem=part_send.at[o],
                recv_sem=part_recv.at[o],
                device_id={"feat": to},
                device_id_type=MESH,
            )

        for o in range(1, nf):
            part_copy(o).start()
        total = part[me]
        for o in range(1, nf):
            part_copy(o).wait()
            total = total + part_in[o]
        unit = total[:vrows, :ncand] / jnp.sqrt(total[:vrows, ncand:2 * ncand] + 1e-06)
        norm = jnp.sqrt(total[vrows:vrows + 1, :ncand] + 1e-06)
        for t in range(vrows // VPT):
            summed = jnp.sum(unit[t * VPT:(t + 1) * VPT], axis=0, keepdims=True)
            out_ref[t:t + 1, :] = summed / VPT / norm


def body(nf, nc, cand_grads, val_grads, second_moment, slot_blocks, slot_seeds):
    L = second_moment.shape[0] // PB
    ncand, nval = cand_grads.shape[0], val_grads.shape[0]
    rows = ncand + nval
    vrows = nc * nval // nf
    steps = L // 2
    f32, bf16, i32 = jnp.float32, jnp.bfloat16, jnp.int32
    VMEM, DMA = pltpu.VMEM, pltpu.SemaphoreType.DMA
    out = pl.pallas_call(
        functools.partial(kernel, nf, nc, L),
        out_shape=jax.ShapeDtypeStruct((vrows // VPT, ncand), f32),
        grid=(steps + 1,),
        in_specs=[
            pl.BlockSpec(memory_space=pltpu.SMEM),
            pl.BlockSpec(slot_blocks.shape, lambda i: (0, 0)),
            pl.BlockSpec(slot_seeds.shape, lambda i: (0, 0)),
            pl.BlockSpec((ncand, 2 * PB), lambda i: (0, jnp.minimum(i, steps - 1))),
            pl.BlockSpec((nval, 2 * PB), lambda i: (0, jnp.minimum(i, steps - 1))),
            pl.BlockSpec((1, 1, 2 * PB), lambda i: (jnp.minimum(i, steps - 1), 0, 0)),
        ],
        out_specs=pl.BlockSpec((vrows // VPT, ncand), lambda i: (0, 0)),
        scratch_shapes=[
            VMEM((PB, LANES), i32),
            VMEM((PB // KC, 2 * rows, KC), bf16),
            VMEM((2, PB // KC, rows, KC), bf16),
            VMEM((2, PB // KC, rows, KC), f32),
            VMEM((steps, PB // KC, rows, KC), f32),
            VMEM((2 * rows, SLOTS * FB), f32),
            VMEM((SLOTS, 2, steps, rows // 2, LANES), f32),
            VMEM((SLOTS, 2, steps, rows // 2, LANES), f32),
            VMEM((ncand, L * FB), f32),
            VMEM((nc, nval, L * FB), f32),
            VMEM((nf, vrows + 8, LANES), f32),
            VMEM((nf, vrows + 8, LANES), f32),
            DMA((2,)), DMA((steps, PB // KC)),
            DMA((SLOTS, 2)), DMA((SLOTS, 2)),
            DMA((nc,)), DMA((nc,)),
            DMA((nf,)), DMA((nf,)),
        ],
        compiler_params=pltpu.CompilerParams(
            collective_id=0, has_side_effects=True, vmem_limit_bytes=56 * 1024 * 1024,
            dimension_semantics=("arbitrary",),
        ),
        cost_estimate=pl.CostEstimate(
            flops=2 * rows * L * PB * SLOTS * FB, bytes_accessed=2 * rows * L * PB, transcendentals=0
        ),
    )(slot_blocks, slot_blocks, slot_seeds, cand_grads, val_grads, second_moment.reshape(steps, 1, 2 * PB))
    return out.T


def solution(mesh):
    placed = (P("cand", "feat"), P("cand", "feat"), P("feat"), P(), P())
    return jax.shard_map(
        functools.partial(body, mesh.shape["feat"], mesh.shape["cand"]),
        mesh=mesh, in_specs=placed, out_specs=P("cand", "feat"), check_vma=False,
    )
```

```python
import functools
import math

import jax
import jax.numpy as jnp
from jax import lax
from jax.experimental import pallas as pl
from jax.experimental.pallas import tpu as pltpu
from jax.sharding import PartitionSpec as P

PB = 8192
FB = 64
SLOTS = 8
VPT = 4
LANES = 128
MESH = pl.DeviceIdType.MESH
C_ROW = 73856093
C_COL = 19349663
C_MIX = 73244475
C_SIGN = ((C_MIX << 15) + (1 << 31)) & 0xFFFFFFFF
C_SIGN = C_SIGN - (1 << 32) if C_SIGN >= (1 << 31) else C_SIGN
KC = 2048
KS = 256
HIGHEST = lax.Precision.HIGHEST


def fold(h):
    return h ^ lax.shift_right_logical(h, jnp.int32(16))


def slot_shift(k, nf):
    stride = nf // SLOTS
    return k * stride if k % 2 == 0 else (k - 1) * stride + 1


def kernel(
    nf, nc, L,
    blocks_ref, map_ref, seeds_ref, cand_ref, val_ref, moment_ref, out_ref,
    table, lhs, own, outgoing, incoming, acc, stage, arrived, mine, val_all, part, part_in,
    grad_send, grad_recv, send_sem, recv_sem, val_send, val_recv, part_send, part_recv,
):
    i = pl.program_id(0)
    steps = L // 2
    me = lax.axis_index("feat")
    col = lax.axis_index("cand")
    core = lax.rem(col, 2)
    other = col + 1 - 2 * core
    ncand = cand_ref.shape[0]
    nval = val_ref.shape[0]
    rows = ncand + nval
    nch = PB // KC

    @pl.when(i == 0)
    def _():
        barrier = pltpu.get_barrier_semaphore()
        for o in range(1, nc):
            pl.semaphore_signal(
                barrier, inc=1, device_id={"cand": lax.rem(col + o, nc)}, device_id_type=MESH
            )
        for o in range(1, nf):
            for c in (col, other):
                pl.semaphore_signal(
                    barrier, inc=1, device_id={"feat": lax.rem(me + o, nf), "cand": c},
                    device_id_type=MESH,
                )

        pl.semaphore_wait(barrier, 2 * (nf - 1) + nc - 1)

    lane = lax.broadcasted_iota(jnp.int32, (1, LANES), 1)
    low = lane < FB

    def adam_part(block, here):
        at = pl.ds(pl.multiple_of(block * PB + here, KS), KS)
        wide = cand_ref[:, at].astype(jnp.float32)
        u = 0.999 * moment_ref[0, :, at] + 0.001 * (wide * wide)
        root = u * lax.rsqrt(u)
        adam = wide * pl.reciprocal(root + 1e-08, approx=True)
        return adam.astype(jnp.bfloat16), val_ref[:, at]

    def grad_copy(step, c):
        slot = lax.rem(step, 2)
        return pltpu.make_async_remote_copy(
            src_ref=outgoing.at[slot, c], dst_ref=incoming.at[step, c],
            send_sem=grad_send.at[slot], recv_sem=grad_recv.at[step, c],
            device_id={"cand": other}, device_id_type=MESH,
        )

    def whole_grad(step):
        slot = lax.rem(step, 2)
        return pltpu.make_async_remote_copy(
            src_ref=outgoing.at[slot], dst_ref=incoming.at[step],
            send_sem=grad_send.at[slot], recv_sem=grad_recv.at[step, 0],
            device_id={"cand": other}, device_id_type=MESH,
        )

    def feature_copy(k, t, pair):
        src = stage.at[k, t] if pair is None else stage.at[k, t, pair]
        dst = arrived.at[k, core] if pair is None else arrived.at[k, core, pair]
        to = lax.rem(me + nf - slot_shift(k, nf), nf)
        return pltpu.make_async_remote_copy(
            src_ref=src, dst_ref=dst,
            send_sem=send_sem.at[k, t], recv_sem=recv_sem.at[k, core],
            device_id={"feat": to, "cand": other if t else col}, device_id_type=MESH,
        )

    @pl.when(i < steps)
    def _():
        slot = lax.rem(i, 2)

        @pl.when(i >= 2)
        def _():
            whole_grad(i - 2).wait_send()

        def prepare(c, carry):
            for s in range(KC // KS):
                here = slice(s * KS, (s + 1) * KS)
                adam, val = adam_part(1 - core, c * KC + s * KS)
                outgoing[slot, c, :ncand, here] = adam.astype(jnp.float32)
                outgoing[slot, c, ncand:, here] = val.astype(jnp.float32)
                adam, val = adam_part(core, c * KC + s * KS)
                own[slot, c, :ncand, here] = adam
                own[slot, c, ncand:, here] = val
            grad_copy(i, c).start()
            return carry

        lax.fori_loop(0, nch, prepare, 0)

        @pl.when(i == 0)
        def _():
            def fill(r, carry):
                base = pl.multiple_of(r * KS, KS)
                p = lax.broadcasted_iota(jnp.int32, (KS, LANES), 0) + base
                f = lax.broadcasted_iota(jnp.int32, (KS, LANES), 1) & (FB - 1)
                table[pl.ds(base, KS), :] = fold((p * jnp.int32(C_ROW)) ^ (f * jnp.int32(C_COL)))
                return carry

            lax.fori_loop(0, PB // KS, fill, 0)


    @pl.when(i > 0)
    def _():
        step = i - 1
        block = 2 * step + core
        slot = lax.rem(step, 2)
        found = map_ref[...] == me * L + block
        picked = jnp.sum(jnp.where(found, seeds_ref[...], 0), axis=1, keepdims=True)
        picked = jnp.broadcast_to(picked, (SLOTS, LANES))
        pair_seeds = []
        for q in range(SLOTS // 2):
            a = picked[2 * q:2 * q + 1]
            b = picked[2 * q + 1:2 * q + 2]
            pair_seeds.append(fold(jnp.where(low, a, b)))

        def gather(c, carry):
            grad_copy(step, c).wait_recv()
            lhs[c, :rows] = own[slot, c]
            lhs[c, rows:] = incoming[step, c].astype(jnp.bfloat16)
            return carry

        lax.fori_loop(0, nch, gather, 0)

        for h in reversed(range(SLOTS // 4)):
            for c in range(nch):
                total = None
                for s in range(KC // KS):
                    here = pl.ds(c * KC + s * KS, KS)
                    sides = []
                    for q in (2 * h, 2 * h + 1):
                        x = (table[here, :] ^ pair_seeds[q]) * jnp.int32(C_MIX)
                        g = fold(x) * jnp.int32(C_SIGN)
                        sides.append(jnp.where(g < 0, 1.0, -1.0).astype(jnp.bfloat16))
                    signs = jnp.concatenate(sides, axis=1)
                    product = jnp.dot(
                        lhs[c, :, s * KS:(s + 1) * KS], signs, preferred_element_type=jnp.float32
                    )
                    total = product if total is None else total + product
                here = slice(h * 256, (h + 1) * 256)
                if c == 0:
                    acc[:, here] = total
                else:
                    acc[:, here] += total
            for q in (2 * h, 2 * h + 1):
                both = acc[:, q * LANES:(q + 1) * LANES]
                turned = pltpu.roll(both, FB, 1)
                for t in (0, 1):
                    top = slice(t * rows, t * rows + rows // 2)
                    end = slice(t * rows + rows // 2, (t + 1) * rows)
                    even_slot = jnp.where(low, both[top], turned[end])
                    odd_slot = jnp.where(low, turned[top], both[end])
                    for k, folded in ((2 * q, even_slot), (2 * q + 1, odd_slot)):
                        if k or t:
                            stage[k, t, step] = folded
                        else:
                            arrived[k, core, step] = folded
            for k in range(4 * h, 4 * h + 4):
                for t in (0, 1):
                    if k or t:
                        feature_copy(k, t, step).start()

    def feature_wait(k, c):
        pltpu.make_async_remote_copy(
            src_ref=stage.at[k, 1], dst_ref=arrived.at[k, c],
            send_sem=send_sem.at[k, 1], recv_sem=recv_sem.at[k, c],
            device_id={"cand": other}, device_id_type=MESH,
        ).wait_recv()

    @pl.when(i == steps)
    def _():
        whole_grad(steps - 2).wait_send()
        whole_grad(steps - 1).wait_send()
        for k in range(SLOTS):
            for t in (0, 1):
                if k or t:
                    feature_copy(k, t, None).wait_send()
            if k:
                feature_wait(k, core)
            feature_wait(k, 1 - core)
        factor = 1.0 / math.sqrt(SLOTS * PB)
        for n in range(L // 2):
            sums = []
            for b in (2 * n, 2 * n + 1):
                total = None
                for k in range(SLOTS):
                    at = lax.rem(blocks_ref[k, me * L + b], jnp.int32(L))
                    term = arrived[k, at & 1, lax.shift_right_logical(at, jnp.int32(1))]
                    total = term if total is None else total + term
                sums.append(total * factor)
            top = jnp.where(low, sums[0], pltpu.roll(sums[1], FB, 1))
            end = jnp.where(low, pltpu.roll(sums[0], FB, 1), sums[1])
            here = slice(n * LANES, (n + 1) * LANES)
            mine[:rows // 2, here] = top
            mine[rows // 2:, here] = end[:ncand - rows // 2]
            val_all[col, :, here] = end[ncand - rows // 2:]

        def val_copy(o):
            return pltpu.make_async_remote_copy(
                src_ref=val_all.at[col],
                dst_ref=val_all.at[col],
                send_sem=val_send.at[o],
                recv_sem=val_recv.at[o],
                device_id={"cand": lax.rem(col + o, nc)},
                device_id_type=MESH,
            )

        for o in range(1, nc):
            val_copy(o).start()
        feats = mine[...]
        ones = jnp.ones((8, L * FB), jnp.float32)
        contract = (((1,), (1,)), ((), ()))
        cand_sq = lax.dot_general(
            ones, feats * feats, contract, precision=HIGHEST, preferred_element_type=jnp.float32
        )
        for o in range(1, nc):
            val_copy(o).wait()
        vals = val_all[...].reshape(nc * nval, L * FB)
        dots = lax.dot_general(
            vals, feats, contract, precision=HIGHEST, preferred_element_type=jnp.float32
        )
        val_sq = jnp.sum(vals * vals, axis=1, keepdims=True)
        vrows = nc * nval // nf
        for t in range(nf):
            here = slice(t * vrows, (t + 1) * vrows)
            part[t, :vrows, :ncand] = dots[here]
            part[t, :vrows, ncand:] = jnp.broadcast_to(val_sq[here], (vrows, LANES - ncand))
            part[t, vrows:, :ncand] = cand_sq
            part[t, vrows:, ncand:] = jnp.zeros((8, LANES - ncand), jnp.float32)

        def part_copy(o):
            to = lax.rem(me + o, nf)
            return pltpu.make_async_remote_copy(
                src_ref=part.at[to],
                dst_ref=part_in.at[o],
                send_sem=part_send.at[o],
                recv_sem=part_recv.at[o],
                device_id={"feat": to},
                device_id_type=MESH,
            )

        for o in range(1, nf):
            part_copy(o).start()
        total = part[me]
        for o in range(1, nf):
            part_copy(o).wait()
            total = total + part_in[o]
        unit = total[:vrows, :ncand] / jnp.sqrt(total[:vrows, ncand:2 * ncand] + 1e-06)
        norm = jnp.sqrt(total[vrows:vrows + 1, :ncand] + 1e-06)
        for t in range(vrows // VPT):
            summed = jnp.sum(unit[t * VPT:(t + 1) * VPT], axis=0, keepdims=True)
            out_ref[t:t + 1, :] = summed / VPT / norm


def body(nf, nc, cand_grads, val_grads, second_moment, slot_blocks, slot_seeds):
    L = second_moment.shape[0] // PB
    ncand, nval = cand_grads.shape[0], val_grads.shape[0]
    rows = ncand + nval
    vrows = nc * nval // nf
    steps = L // 2
    f32, bf16, i32 = jnp.float32, jnp.bfloat16, jnp.int32
    VMEM, DMA = pltpu.VMEM, pltpu.SemaphoreType.DMA
    out = pl.pallas_call(
        functools.partial(kernel, nf, nc, L),
        out_shape=jax.ShapeDtypeStruct((vrows // VPT, ncand), f32),
        grid=(steps + 1,),
        in_specs=[
            pl.BlockSpec(memory_space=pltpu.SMEM),
            pl.BlockSpec(slot_blocks.shape, lambda i: (0, 0)),
            pl.BlockSpec(slot_seeds.shape, lambda i: (0, 0)),
            pl.BlockSpec((ncand, 2 * PB), lambda i: (0, jnp.minimum(i, steps - 1))),
            pl.BlockSpec((nval, 2 * PB), lambda i: (0, jnp.minimum(i, steps - 1))),
            pl.BlockSpec((1, 1, 2 * PB), lambda i: (jnp.minimum(i, steps - 1), 0, 0)),
        ],
        out_specs=pl.BlockSpec((vrows // VPT, ncand), lambda i: (0, 0)),
        scratch_shapes=[
            VMEM((PB, LANES), i32),
            VMEM((PB // KC, 2 * rows, KC), bf16),
            VMEM((2, PB // KC, rows, KC), bf16),
            VMEM((2, PB // KC, rows, KC), f32),
            VMEM((steps, PB // KC, rows, KC), f32),
            VMEM((2 * rows, SLOTS * FB), f32),
            VMEM((SLOTS, 2, steps, rows // 2, LANES), f32),
            VMEM((SLOTS, 2, steps, rows // 2, LANES), f32),
            VMEM((ncand, L * FB), f32),
            VMEM((nc, nval, L * FB), f32),
            VMEM((nf, vrows + 8, LANES), f32),
            VMEM((nf, vrows + 8, LANES), f32),
            DMA((2,)), DMA((steps, PB // KC)),
            DMA((SLOTS, 2)), DMA((SLOTS, 2)),
            DMA((nc,)), DMA((nc,)),
            DMA((nf,)), DMA((nf,)),
        ],
        compiler_params=pltpu.CompilerParams(
            collective_id=0, has_side_effects=True, vmem_limit_bytes=56 * 1024 * 1024,
            dimension_semantics=("arbitrary",),
        ),
        cost_estimate=pl.CostEstimate(
            flops=2 * rows * L * PB * SLOTS * FB, bytes_accessed=2 * rows * L * PB, transcendentals=0
        ),
    )(slot_blocks, slot_blocks, slot_seeds, cand_grads, val_grads, second_moment.reshape(steps, 1, 2 * PB))
    return out.T


def solution(mesh):
    placed = (P("cand", "feat"), P("cand", "feat"), P("feat"), P(), P())
    return jax.shard_map(
        functools.partial(body, mesh.shape["feat"], mesh.shape["cand"]),
        mesh=mesh, in_specs=placed, out_specs=P("cand", "feat"), check_vma=False,
    )
```

```python
import functools
import math

import jax
import jax.numpy as jnp
from jax import lax
from jax.experimental import pallas as pl
from jax.experimental.pallas import tpu as pltpu
from jax.sharding import PartitionSpec as P

PB = 8192
FB = 64
SLOTS = 8
VPT = 4
LANES = 128
MESH = pl.DeviceIdType.MESH
C_ROW = 73856093
C_COL = 19349663
C_MIX = 73244475
C_SIGN = ((C_MIX << 15) + (1 << 31)) & 0xFFFFFFFF
C_SIGN = C_SIGN - (1 << 32) if C_SIGN >= (1 << 31) else C_SIGN
KC = 2048
KS = 256
HIGHEST = lax.Precision.HIGHEST


def fold(h):
    return h ^ lax.shift_right_logical(h, jnp.int32(16))


def slot_shift(k, nf):
    stride = nf // SLOTS
    return k * stride if k % 2 == 0 else (k - 1) * stride + 1


def kernel(
    nf, nc, L,
    blocks_ref, map_ref, seeds_ref, cand_ref, val_ref, moment_ref, out_ref,
    table, lhs, own, outgoing, incoming, signs, acc, stage, arrived, mine, val_all, part, part_in,
    grad_send, grad_recv, send_sem, recv_sem, val_send, val_recv, part_send, part_recv,
):
    i = pl.program_id(0)
    steps = L // 2
    me = lax.axis_index("feat")
    col = lax.axis_index("cand")
    core = lax.rem(col, 2)
    other = col + 1 - 2 * core
    ncand = cand_ref.shape[0]
    nval = val_ref.shape[0]
    rows = ncand + nval
    nch = PB // KC

    @pl.when(i == 0)
    def _():
        barrier = pltpu.get_barrier_semaphore()
        for o in range(1, nc):
            pl.semaphore_signal(
                barrier, inc=1, device_id={"cand": lax.rem(col + o, nc)}, device_id_type=MESH
            )
        for o in range(1, nf):
            for c in (col, other):
                pl.semaphore_signal(
                    barrier, inc=1, device_id={"feat": lax.rem(me + o, nf), "cand": c},
                    device_id_type=MESH,
                )

        pl.semaphore_wait(barrier, 2 * (nf - 1) + nc - 1)

    lane = lax.broadcasted_iota(jnp.int32, (1, LANES), 1)
    low = lane < FB

    def adam_part(block, here):
        at = pl.ds(pl.multiple_of(block * PB + here, KS), KS)
        wide = cand_ref[:, at].astype(jnp.float32)
        u = 0.999 * moment_ref[0, :, at] + 0.001 * (wide * wide)
        root = u * lax.rsqrt(u)
        adam = wide * pl.reciprocal(root + 1e-08, approx=True)
        return adam.astype(jnp.bfloat16), val_ref[:, at]

    def grad_copy(step, c):
        slot = lax.rem(step, 2)
        return pltpu.make_async_remote_copy(
            src_ref=outgoing.at[slot, c], dst_ref=incoming.at[step, c],
            send_sem=grad_send.at[slot], recv_sem=grad_recv.at[step, c],
            device_id={"cand": other}, device_id_type=MESH,
        )

    def whole_grad(step):
        slot = lax.rem(step, 2)
        return pltpu.make_async_remote_copy(
            src_ref=outgoing.at[slot], dst_ref=incoming.at[step],
            send_sem=grad_send.at[slot], recv_sem=grad_recv.at[step, 0],
            device_id={"cand": other}, device_id_type=MESH,
        )

    def feature_copy(k, t, pair):
        src = stage.at[k, t] if pair is None else stage.at[k, t, pair]
        dst = arrived.at[k, core] if pair is None else arrived.at[k, core, pair]
        to = lax.rem(me + nf - slot_shift(k, nf), nf)
        return pltpu.make_async_remote_copy(
            src_ref=src, dst_ref=dst,
            send_sem=send_sem.at[k, t], recv_sem=recv_sem.at[k, core],
            device_id={"feat": to, "cand": other if t else col}, device_id_type=MESH,
        )

    @pl.when(i < steps)
    def _():
        slot = lax.rem(i, 2)

        @pl.when(i >= 2)
        def _():
            whole_grad(i - 2).wait_send()

        def prepare(c, carry):
            for s in range(KC // KS):
                here = slice(s * KS, (s + 1) * KS)
                adam, val = adam_part(1 - core, c * KC + s * KS)
                outgoing[slot, c, :ncand, here] = adam.astype(jnp.float32)
                outgoing[slot, c, ncand:, here] = val.astype(jnp.float32)
                adam, val = adam_part(core, c * KC + s * KS)
                own[slot, c, :ncand, here] = adam
                own[slot, c, ncand:, here] = val
            grad_copy(i, c).start()
            return carry

        lax.fori_loop(0, nch, prepare, 0)

        @pl.when(i == 0)
        def _():
            def fill(r, carry):
                base = pl.multiple_of(r * KS, KS)
                p = lax.broadcasted_iota(jnp.int32, (KS, LANES), 0) + base
                f = lax.broadcasted_iota(jnp.int32, (KS, LANES), 1) & (FB - 1)
                table[pl.ds(base, KS), :] = fold((p * jnp.int32(C_ROW)) ^ (f * jnp.int32(C_COL)))
                return carry

            lax.fori_loop(0, PB // KS, fill, 0)


    @pl.when(i > 0)
    def _():
        step = i - 1
        block = 2 * step + core
        slot = lax.rem(step, 2)
        found = map_ref[...] == me * L + block
        picked = jnp.sum(jnp.where(found, seeds_ref[...], 0), axis=1, keepdims=True)
        picked = jnp.broadcast_to(picked, (SLOTS, LANES))
        pair_seeds = []
        for q in range(SLOTS // 2):
            a = picked[2 * q:2 * q + 1]
            b = picked[2 * q + 1:2 * q + 2]
            pair_seeds.append(fold(jnp.where(low, a, b)))

        def gather(c, carry):
            grad_copy(step, c).wait_recv()
            lhs[c, :rows] = own[slot, c]
            lhs[c, rows:] = incoming[step, c].astype(jnp.bfloat16)
            return carry

        lax.fori_loop(0, nch, gather, 0)

        for h in reversed(range(SLOTS // 4)):
            for c in range(nch):
                for s in range(KC // KS):
                    here = slice(s * KS, (s + 1) * KS)
                    rows_here = pl.ds(c * KC + s * KS, KS)
                    for n, q in enumerate((2 * h, 2 * h + 1)):
                        x = (table[rows_here, :] ^ pair_seeds[q]) * jnp.int32(C_MIX)
                        g = fold(x) * jnp.int32(C_SIGN)
                        signs[c % 2, here, n * LANES:(n + 1) * LANES] = jnp.where(
                            g < 0, 1.0, -1.0
                        ).astype(jnp.bfloat16)
                total = jnp.dot(lhs[c], signs[c % 2], preferred_element_type=jnp.float32)
                here = slice(h * 256, (h + 1) * 256)
                if c == 0:
                    acc[:, here] = total
                else:
                    acc[:, here] += total
            for q in (2 * h, 2 * h + 1):
                both = acc[:, q * LANES:(q + 1) * LANES]
                turned = pltpu.roll(both, FB, 1)
                for t in (0, 1):
                    top = slice(t * rows, t * rows + rows // 2)
                    end = slice(t * rows + rows // 2, (t + 1) * rows)
                    even_slot = jnp.where(low, both[top], turned[end])
                    odd_slot = jnp.where(low, turned[top], both[end])
                    for k, folded in ((2 * q, even_slot), (2 * q + 1, odd_slot)):
                        if k or t:
                            stage[k, t, step] = folded
                        else:
                            arrived[k, core, step] = folded
            for k in range(4 * h, 4 * h + 4):
                for t in (0, 1):
                    if k or t:
                        feature_copy(k, t, step).start()

    def feature_wait(k, c):
        pltpu.make_async_remote_copy(
            src_ref=stage.at[k, 1], dst_ref=arrived.at[k, c],
            send_sem=send_sem.at[k, 1], recv_sem=recv_sem.at[k, c],
            device_id={"cand": other}, device_id_type=MESH,
        ).wait_recv()

    @pl.when(i == steps)
    def _():
        whole_grad(steps - 2).wait_send()
        whole_grad(steps - 1).wait_send()
        for k in range(SLOTS):
            for t in (0, 1):
                if k or t:
                    feature_copy(k, t, None).wait_send()
            if k:
                feature_wait(k, core)
            feature_wait(k, 1 - core)
        factor = 1.0 / math.sqrt(SLOTS * PB)
        for n in range(L // 2):
            sums = []
            for b in (2 * n, 2 * n + 1):
                total = None
                for k in range(SLOTS):
                    at = lax.rem(blocks_ref[k, me * L + b], jnp.int32(L))
                    term = arrived[k, at & 1, lax.shift_right_logical(at, jnp.int32(1))]
                    total = term if total is None else total + term
                sums.append(total * factor)
            top = jnp.where(low, sums[0], pltpu.roll(sums[1], FB, 1))
            end = jnp.where(low, pltpu.roll(sums[0], FB, 1), sums[1])
            here = slice(n * LANES, (n + 1) * LANES)
            mine[:rows // 2, here] = top
            mine[rows // 2:, here] = end[:ncand - rows // 2]
            val_all[col, :, here] = end[ncand - rows // 2:]

        def val_copy(o):
            return pltpu.make_async_remote_copy(
                src_ref=val_all.at[col],
                dst_ref=val_all.at[col],
                send_sem=val_send.at[o],
                recv_sem=val_recv.at[o],
                device_id={"cand": lax.rem(col + o, nc)},
                device_id_type=MESH,
            )

        for o in range(1, nc):
            val_copy(o).start()
        feats = mine[...]
        ones = jnp.ones((8, L * FB), jnp.float32)
        contract = (((1,), (1,)), ((), ()))
        cand_sq = lax.dot_general(
            ones, feats * feats, contract, precision=HIGHEST, preferred_element_type=jnp.float32
        )
        for o in range(1, nc):
            val_copy(o).wait()
        vals = val_all[...].reshape(nc * nval, L * FB)
        dots = lax.dot_general(
            vals, feats, contract, precision=HIGHEST, preferred_element_type=jnp.float32
        )
        val_sq = jnp.sum(vals * vals, axis=1, keepdims=True)
        vrows = nc * nval // nf
        for t in range(nf):
            here = slice(t * vrows, (t + 1) * vrows)
            part[t, :vrows, :ncand] = dots[here]
            part[t, :vrows, ncand:] = jnp.broadcast_to(val_sq[here], (vrows, LANES - ncand))
            part[t, vrows:, :ncand] = cand_sq
            part[t, vrows:, ncand:] = jnp.zeros((8, LANES - ncand), jnp.float32)

        def part_copy(o):
            to = lax.rem(me + o, nf)
            return pltpu.make_async_remote_copy(
                src_ref=part.at[to],
                dst_ref=part_in.at[o],
                send_sem=part_send.at[o],
                recv_sem=part_recv.at[o],
                device_id={"feat": to},
                device_id_type=MESH,
            )

        for o in range(1, nf):
            part_copy(o).start()
        total = part[me]
        for o in range(1, nf):
            part_copy(o).wait()
            total = total + part_in[o]
        unit = total[:vrows, :ncand] / jnp.sqrt(total[:vrows, ncand:2 * ncand] + 1e-06)
        norm = jnp.sqrt(total[vrows:vrows + 1, :ncand] + 1e-06)
        for t in range(vrows // VPT):
            summed = jnp.sum(unit[t * VPT:(t + 1) * VPT], axis=0, keepdims=True)
            out_ref[t:t + 1, :] = summed / VPT / norm


def body(nf, nc, cand_grads, val_grads, second_moment, slot_blocks, slot_seeds):
    L = second_moment.shape[0] // PB
    ncand, nval = cand_grads.shape[0], val_grads.shape[0]
    rows = ncand + nval
    vrows = nc * nval // nf
    steps = L // 2
    f32, bf16, i32 = jnp.float32, jnp.bfloat16, jnp.int32
    VMEM, DMA = pltpu.VMEM, pltpu.SemaphoreType.DMA
    out = pl.pallas_call(
        functools.partial(kernel, nf, nc, L),
        out_shape=jax.ShapeDtypeStruct((vrows // VPT, ncand), f32),
        grid=(steps + 1,),
        in_specs=[
            pl.BlockSpec(memory_space=pltpu.SMEM),
            pl.BlockSpec(slot_blocks.shape, lambda i: (0, 0)),
            pl.BlockSpec(slot_seeds.shape, lambda i: (0, 0)),
            pl.BlockSpec((ncand, 2 * PB), lambda i: (0, jnp.minimum(i, steps - 1))),
            pl.BlockSpec((nval, 2 * PB), lambda i: (0, jnp.minimum(i, steps - 1))),
            pl.BlockSpec((1, 1, 2 * PB), lambda i: (jnp.minimum(i, steps - 1), 0, 0)),
        ],
        out_specs=pl.BlockSpec((vrows // VPT, ncand), lambda i: (0, 0)),
        scratch_shapes=[
            VMEM((PB, LANES), i32),
            VMEM((PB // KC, 2 * rows, KC), bf16),
            VMEM((2, PB // KC, rows, KC), bf16),
            VMEM((2, PB // KC, rows, KC), f32),
            VMEM((steps, PB // KC, rows, KC), f32),
            VMEM((2, KC, 2 * LANES), bf16),
            VMEM((2 * rows, SLOTS * FB), f32),
            VMEM((SLOTS, 2, steps, rows // 2, LANES), f32),
            VMEM((SLOTS, 2, steps, rows // 2, LANES), f32),
            VMEM((ncand, L * FB), f32),
            VMEM((nc, nval, L * FB), f32),
            VMEM((nf, vrows + 8, LANES), f32),
            VMEM((nf, vrows + 8, LANES), f32),
            DMA((2,)), DMA((steps, PB // KC)),
            DMA((SLOTS, 2)), DMA((SLOTS, 2)),
            DMA((nc,)), DMA((nc,)),
            DMA((nf,)), DMA((nf,)),
        ],
        compiler_params=pltpu.CompilerParams(
            collective_id=0, has_side_effects=True, vmem_limit_bytes=56 * 1024 * 1024,
            dimension_semantics=("arbitrary",),
        ),
        cost_estimate=pl.CostEstimate(
            flops=2 * rows * L * PB * SLOTS * FB, bytes_accessed=2 * rows * L * PB, transcendentals=0
        ),
    )(slot_blocks, slot_blocks, slot_seeds, cand_grads, val_grads, second_moment.reshape(steps, 1, 2 * PB))
    return out.T


def solution(mesh):
    placed = (P("cand", "feat"), P("cand", "feat"), P("feat"), P(), P())
    return jax.shard_map(
        functools.partial(body, mesh.shape["feat"], mesh.shape["cand"]),
        mesh=mesh, in_specs=placed, out_specs=P("cand", "feat"), check_vma=False,
    )
```

```python
import functools
import math

import jax
import jax.numpy as jnp
from jax import lax
from jax.experimental import pallas as pl
from jax.experimental.pallas import tpu as pltpu
from jax.sharding import PartitionSpec as P

PB = 8192
FB = 64
SLOTS = 8
VPT = 4
LANES = 128
MESH = pl.DeviceIdType.MESH
C_ROW = 73856093
C_COL = 19349663
C_MIX = 73244475
C_SIGN = ((C_MIX << 15) + (1 << 31)) & 0xFFFFFFFF
C_SIGN = C_SIGN - (1 << 32) if C_SIGN >= (1 << 31) else C_SIGN
KC = 2048
KS = 512
HIGHEST = lax.Precision.HIGHEST


def fold(h):
    return h ^ lax.shift_right_logical(h, jnp.int32(16))


def slot_shift(k, nf):
    stride = nf // SLOTS
    return k * stride if k % 2 == 0 else (k - 1) * stride + 1


def kernel(
    nf, nc, L,
    blocks_ref, map_ref, seeds_ref, cand_ref, val_ref, moment_ref, out_ref,
    table, lhs, own, outgoing, incoming, acc, stage, arrived, mine, val_all, part, part_in,
    grad_send, grad_recv, send_sem, recv_sem, val_send, val_recv, part_send, part_recv,
):
    i = pl.program_id(0)
    steps = L // 2
    me = lax.axis_index("feat")
    col = lax.axis_index("cand")
    core = lax.rem(col, 2)
    other = col + 1 - 2 * core
    ncand = cand_ref.shape[0]
    nval = val_ref.shape[0]
    rows = ncand + nval
    nch = PB // KC

    @pl.when(i == 0)
    def _():
        barrier = pltpu.get_barrier_semaphore()
        for o in range(1, nc):
            pl.semaphore_signal(
                barrier, inc=1, device_id={"cand": lax.rem(col + o, nc)}, device_id_type=MESH
            )
        for o in range(1, nf):
            for c in (col, other):
                pl.semaphore_signal(
                    barrier, inc=1, device_id={"feat": lax.rem(me + o, nf), "cand": c},
                    device_id_type=MESH,
                )

        pl.semaphore_wait(barrier, 2 * (nf - 1) + nc - 1)

    lane = lax.broadcasted_iota(jnp.int32, (1, LANES), 1)
    low = lane < FB

    def adam_part(block, here):
        at = pl.ds(pl.multiple_of(block * PB + here, KS), KS)
        wide = cand_ref[:, at].astype(jnp.float32)
        u = 0.999 * moment_ref[0, :, at] + 0.001 * (wide * wide)
        root = u * lax.rsqrt(u)
        adam = wide * pl.reciprocal(root + 1e-08, approx=True)
        return adam.astype(jnp.bfloat16), val_ref[:, at]

    def grad_copy(step, c):
        slot = lax.rem(step, 2)
        return pltpu.make_async_remote_copy(
            src_ref=outgoing.at[slot, c], dst_ref=incoming.at[step, c],
            send_sem=grad_send.at[slot], recv_sem=grad_recv.at[step, c],
            device_id={"cand": other}, device_id_type=MESH,
        )

    def whole_grad(step):
        slot = lax.rem(step, 2)
        return pltpu.make_async_remote_copy(
            src_ref=outgoing.at[slot], dst_ref=incoming.at[step],
            send_sem=grad_send.at[slot], recv_sem=grad_recv.at[step, 0],
            device_id={"cand": other}, device_id_type=MESH,
        )

    def feature_copy(k, t, pair):
        src = stage.at[k, t] if pair is None else stage.at[k, t, pair]
        dst = arrived.at[k, core] if pair is None else arrived.at[k, core, pair]
        to = lax.rem(me + nf - slot_shift(k, nf), nf)
        return pltpu.make_async_remote_copy(
            src_ref=src, dst_ref=dst,
            send_sem=send_sem.at[k, t], recv_sem=recv_sem.at[k, core],
            device_id={"feat": to, "cand": other if t else col}, device_id_type=MESH,
        )

    @pl.when(i < steps)
    def _():
        slot = lax.rem(i, 2)

        @pl.when(i >= 2)
        def _():
            whole_grad(i - 2).wait_send()

        def prepare(c, carry):
            for s in range(KC // KS):
                here = slice(s * KS, (s + 1) * KS)
                adam, val = adam_part(1 - core, c * KC + s * KS)
                outgoing[slot, c, :ncand, here] = adam.astype(jnp.float32)
                outgoing[slot, c, ncand:, here] = val.astype(jnp.float32)
                adam, val = adam_part(core, c * KC + s * KS)
                own[slot, c, :ncand, here] = adam
                own[slot, c, ncand:, here] = val
            grad_copy(i, c).start()
            return carry

        lax.fori_loop(0, nch, prepare, 0)

        @pl.when(i == 0)
        def _():
            def fill(r, carry):
                base = pl.multiple_of(r * KS, KS)
                p = lax.broadcasted_iota(jnp.int32, (KS, LANES), 0) + base
                f = lax.broadcasted_iota(jnp.int32, (KS, LANES), 1) & (FB - 1)
                table[pl.ds(base, KS), :] = fold((p * jnp.int32(C_ROW)) ^ (f * jnp.int32(C_COL)))
                return carry

            lax.fori_loop(0, PB // KS, fill, 0)


    @pl.when(i > 0)
    def _():
        step = i - 1
        block = 2 * step + core
        slot = lax.rem(step, 2)
        found = map_ref[...] == me * L + block
        picked = jnp.sum(jnp.where(found, seeds_ref[...], 0), axis=1, keepdims=True)
        picked = jnp.broadcast_to(picked, (SLOTS, LANES))
        pair_seeds = []
        for q in range(SLOTS // 2):
            a = picked[2 * q:2 * q + 1]
            b = picked[2 * q + 1:2 * q + 2]
            pair_seeds.append(fold(jnp.where(low, a, b)))

        def gather(c, carry):
            grad_copy(step, c).wait_recv()
            lhs[c, :rows] = own[slot, c]
            lhs[c, rows:] = incoming[step, c].astype(jnp.bfloat16)
            return carry

        lax.fori_loop(0, nch, gather, 0)

        for h in reversed(range(SLOTS // 4)):
            for c in range(nch):
                total = None
                for s in range(KC // KS):
                    here = pl.ds(c * KC + s * KS, KS)
                    sides = []
                    for q in (2 * h, 2 * h + 1):
                        x = (table[here, :] ^ pair_seeds[q]) * jnp.int32(C_MIX)
                        g = fold(x) * jnp.int32(C_SIGN)
                        sides.append(jnp.where(g < 0, 1.0, -1.0).astype(jnp.bfloat16))
                    signs = jnp.concatenate(sides, axis=1)
                    product = jnp.dot(
                        lhs[c, :, s * KS:(s + 1) * KS], signs, preferred_element_type=jnp.float32
                    )
                    total = product if total is None else total + product
                here = slice(h * 256, (h + 1) * 256)
                if c == 0:
                    acc[:, here] = total
                else:
                    acc[:, here] += total
            for q in (2 * h, 2 * h + 1):
                both = acc[:, q * LANES:(q + 1) * LANES]
                turned = pltpu.roll(both, FB, 1)
                for t in (0, 1):
                    top = slice(t * rows, t * rows + rows // 2)
                    end = slice(t * rows + rows // 2, (t + 1) * rows)
                    even_slot = jnp.where(low, both[top], turned[end])
                    odd_slot = jnp.where(low, turned[top], both[end])
                    for k, folded in ((2 * q, even_slot), (2 * q + 1, odd_slot)):
                        if k or t:
                            stage[k, t, step] = folded
                        else:
                            arrived[k, core, step] = folded
            for k in range(4 * h, 4 * h + 4):
                for t in (0, 1):
                    if k or t:
                        feature_copy(k, t, step).start()

    def feature_wait(k, c):
        pltpu.make_async_remote_copy(
            src_ref=stage.at[k, 1], dst_ref=arrived.at[k, c],
            send_sem=send_sem.at[k, 1], recv_sem=recv_sem.at[k, c],
            device_id={"cand": other}, device_id_type=MESH,
        ).wait_recv()

    @pl.when(i == steps)
    def _():
        whole_grad(steps - 2).wait_send()
        whole_grad(steps - 1).wait_send()
        for k in range(SLOTS):
            for t in (0, 1):
                if k or t:
                    feature_copy(k, t, None).wait_send()
            if k:
                feature_wait(k, core)
            feature_wait(k, 1 - core)
        factor = 1.0 / math.sqrt(SLOTS * PB)
        for n in range(L // 2):
            sums = []
            for b in (2 * n, 2 * n + 1):
                total = None
                for k in range(SLOTS):
                    at = lax.rem(blocks_ref[k, me * L + b], jnp.int32(L))
                    term = arrived[k, at & 1, lax.shift_right_logical(at, jnp.int32(1))]
                    total = term if total is None else total + term
                sums.append(total * factor)
            top = jnp.where(low, sums[0], pltpu.roll(sums[1], FB, 1))
            end = jnp.where(low, pltpu.roll(sums[0], FB, 1), sums[1])
            here = slice(n * LANES, (n + 1) * LANES)
            mine[:rows // 2, here] = top
            mine[rows // 2:, here] = end[:ncand - rows // 2]
            val_all[col, :, here] = end[ncand - rows // 2:]

        def val_copy(o):
            return pltpu.make_async_remote_copy(
                src_ref=val_all.at[col],
                dst_ref=val_all.at[col],
                send_sem=val_send.at[o],
                recv_sem=val_recv.at[o],
                device_id={"cand": lax.rem(col + o, nc)},
                device_id_type=MESH,
            )

        for o in range(1, nc):
            val_copy(o).start()
        feats = mine[...]
        ones = jnp.ones((8, L * FB), jnp.float32)
        contract = (((1,), (1,)), ((), ()))
        cand_sq = lax.dot_general(
            ones, feats * feats, contract, precision=HIGHEST, preferred_element_type=jnp.float32
        )
        for o in range(1, nc):
            val_copy(o).wait()
        vals = val_all[...].reshape(nc * nval, L * FB)
        dots = lax.dot_general(
            vals, feats, contract, precision=HIGHEST, preferred_element_type=jnp.float32
        )
        val_sq = jnp.sum(vals * vals, axis=1, keepdims=True)
        vrows = nc * nval // nf
        for t in range(nf):
            here = slice(t * vrows, (t + 1) * vrows)
            part[t, :vrows, :ncand] = dots[here]
            part[t, :vrows, ncand:] = jnp.broadcast_to(val_sq[here], (vrows, LANES - ncand))
            part[t, vrows:, :ncand] = cand_sq
            part[t, vrows:, ncand:] = jnp.zeros((8, LANES - ncand), jnp.float32)

        def part_copy(o):
            to = lax.rem(me + o, nf)
            return pltpu.make_async_remote_copy(
                src_ref=part.at[to],
                dst_ref=part_in.at[o],
                send_sem=part_send.at[o],
                recv_sem=part_recv.at[o],
                device_id={"feat": to},
                device_id_type=MESH,
            )

        for o in range(1, nf):
            part_copy(o).start()
        total = part[me]
        for o in range(1, nf):
            part_copy(o).wait()
            total = total + part_in[o]
        unit = total[:vrows, :ncand] / jnp.sqrt(total[:vrows, ncand:2 * ncand] + 1e-06)
        norm = jnp.sqrt(total[vrows:vrows + 1, :ncand] + 1e-06)
        for t in range(vrows // VPT):
            summed = jnp.sum(unit[t * VPT:(t + 1) * VPT], axis=0, keepdims=True)
            out_ref[t:t + 1, :] = summed / VPT / norm


def body(nf, nc, cand_grads, val_grads, second_moment, slot_blocks, slot_seeds):
    L = second_moment.shape[0] // PB
    ncand, nval = cand_grads.shape[0], val_grads.shape[0]
    rows = ncand + nval
    vrows = nc * nval // nf
    steps = L // 2
    f32, bf16, i32 = jnp.float32, jnp.bfloat16, jnp.int32
    VMEM, DMA = pltpu.VMEM, pltpu.SemaphoreType.DMA
    out = pl.pallas_call(
        functools.partial(kernel, nf, nc, L),
        out_shape=jax.ShapeDtypeStruct((vrows // VPT, ncand), f32),
        grid=(steps + 1,),
        in_specs=[
            pl.BlockSpec(memory_space=pltpu.SMEM),
            pl.BlockSpec(slot_blocks.shape, lambda i: (0, 0)),
            pl.BlockSpec(slot_seeds.shape, lambda i: (0, 0)),
            pl.BlockSpec((ncand, 2 * PB), lambda i: (0, jnp.minimum(i, steps - 1))),
            pl.BlockSpec((nval, 2 * PB), lambda i: (0, jnp.minimum(i, steps - 1))),
            pl.BlockSpec((1, 1, 2 * PB), lambda i: (jnp.minimum(i, steps - 1), 0, 0)),
        ],
        out_specs=pl.BlockSpec((vrows // VPT, ncand), lambda i: (0, 0)),
        scratch_shapes=[
            VMEM((PB, LANES), i32),
            VMEM((PB // KC, 2 * rows, KC), bf16),
            VMEM((2, PB // KC, rows, KC), bf16),
            VMEM((2, PB // KC, rows, KC), f32),
            VMEM((steps, PB // KC, rows, KC), f32),
            VMEM((2 * rows, SLOTS * FB), f32),
            VMEM((SLOTS, 2, steps, rows // 2, LANES), f32),
            VMEM((SLOTS, 2, steps, rows // 2, LANES), f32),
            VMEM((ncand, L * FB), f32),
            VMEM((nc, nval, L * FB), f32),
            VMEM((nf, vrows + 8, LANES), f32),
            VMEM((nf, vrows + 8, LANES), f32),
            DMA((2,)), DMA((steps, PB // KC)),
            DMA((SLOTS, 2)), DMA((SLOTS, 2)),
            DMA((nc,)), DMA((nc,)),
            DMA((nf,)), DMA((nf,)),
        ],
        compiler_params=pltpu.CompilerParams(
            collective_id=0, has_side_effects=True, vmem_limit_bytes=56 * 1024 * 1024,
            dimension_semantics=("arbitrary",),
        ),
        cost_estimate=pl.CostEstimate(
            flops=2 * rows * L * PB * SLOTS * FB, bytes_accessed=2 * rows * L * PB, transcendentals=0
        ),
    )(slot_blocks, slot_blocks, slot_seeds, cand_grads, val_grads, second_moment.reshape(steps, 1, 2 * PB))
    return out.T


def solution(mesh):
    placed = (P("cand", "feat"), P("cand", "feat"), P("feat"), P(), P())
    return jax.shard_map(
        functools.partial(body, mesh.shape["feat"], mesh.shape["cand"]),
        mesh=mesh, in_specs=placed, out_specs=P("cand", "feat"), check_vma=False,
    )
```
